128 devices in a mesh: slab: 32 (over z, x, core), sub: 4 (over y).
Axes of the slice: x: 4, y: 4, z: 4, core: 2. Of those that a mesh axis runs over, the one named last changes fastest.
Arguments:
- starts: float32 [32, 8, 2048, 128], P('slab', 'sub'), may hold values from -6 to 6
- sources: bfloat16 [32, 8, 2048, 128], P('slab', 'sub'), may hold values from -6 to 6
- inverse_conductance: bfloat16 [8, 2048, 2048], P('sub'), as said below
- coarse_decay: float32 [32, 8, 2048], P('slab', 'sub'), as said below
- interface_nodes: int32 [8, 256], P('sub'), may hold values from 0 to 2047, as said below
- retire: int32 [128], replicated, may hold values from 0 to 2, as said below
Outputs:
- window: float32 [32, 8, 2048, 128], P('slab', 'sub')
The draws below stay inside these ranges and needn't reach their ends.
Inputs may be any that keep to these rules, and one draw needn't show every extreme that they name: `interface_nodes`: within each subnetwork the interface nodes are distinct, and 0 and 2047 are in every subnetwork's list. `retire`: some case retires no slab and some retires 2. `coarse_decay`: entries lie in (0, 1]. `inverse_conductance`: each matrix has a positive diagonal.
All inputs are finite; a program needn't handle non-finite values.
Results may differ from the reference program's by a relative error of at most 0.0042.
Values sent between devices are 32-bit elements; how exact they have to be, the bound alone decides.
A program may use at most 192 MiB of HBM per device.

```python
import jax
import jax.numpy as jnp
from jax import lax

GRID_NODES = 2048
GRID_SUBNETWORKS = 8
CASES = 128
IFACE = 256
STEPS = 8
TIME_SLABS = 32
RMAX = 2


def draw_inverse_conductance(key, part):
    first, second = jax.random.split(key)
    spread = 0.2
    diagonal = jax.random.uniform(first, (GRID_SUBNETWORKS, GRID_NODES), jnp.float32, 0.6, 0.9)
    offdiag = jax.random.normal(second, (GRID_SUBNETWORKS, GRID_NODES, GRID_NODES), jnp.float32) * (spread / GRID_NODES ** 0.5)
    eye = jnp.eye(GRID_NODES, dtype=jnp.float32)
    return (offdiag + diagonal[:, :, None] * eye[None]).astype(jnp.bfloat16)


def draw_coarse_decay(key, part):
    random_keys = jax.random.split(key, 4)
    low = jnp.log(0.1 / TIME_SLABS)
    high = jnp.log(3.0)
    decay_rates = jnp.exp(jax.random.uniform(random_keys[0], (GRID_SUBNETWORKS, GRID_NODES), jnp.float32, low, high))
    random_perturbation = jax.random.uniform(random_keys[1], (TIME_SLABS, GRID_SUBNETWORKS, GRID_NODES), jnp.float32, 0.6, 1.6)
    surge_instant = jax.random.randint(random_keys[2], (2, GRID_SUBNETWORKS, GRID_NODES), 0, TIME_SLABS)
    scale_factor = jax.random.uniform(random_keys[3], (GRID_SUBNETWORKS, GRID_NODES), jnp.float32, 0.5, 0.8)
    slab_indices = jnp.arange(TIME_SLABS)[:, None, None]
    struck_mask = (slab_indices == surge_instant[0][None]) | (slab_indices == surge_instant[1][None])
    surge_pulse = jnp.where(struck_mask, scale_factor[None], 1.0)
    return jnp.exp(-decay_rates[None] * random_perturbation) * surge_pulse


def draw_interface_nodes(key, part):

    def single(sub_key):
        first, second = jax.random.split(sub_key)
        inner = jax.random.permutation(first, GRID_NODES - 2)[:IFACE - 2] + 1
        whole = jnp.concatenate([jnp.array([0, GRID_NODES - 1], dtype=jnp.int32), inner.astype(jnp.int32)])
        order = jax.random.permutation(second, IFACE)
        return whole[order].astype(jnp.int32)
    return jax.vmap(single)(jax.random.split(jax.random.fold_in(key, 11), GRID_SUBNETWORKS))


def draw_retire(key, part):
    first, second = jax.random.split(jax.random.fold_in(key, 23))
    values = jax.random.randint(first, (CASES,), 0, RMAX + 1)
    order = jax.random.permutation(second, CASES)
    values = values.at[order[0]].set(0).at[order[1]].set(RMAX)
    return values.astype(jnp.int32)


def level_of(rng, dims, cuts, smallest, top_value):
    def one(axis_at, shards_of):
        draws = jax.random.uniform(jax.random.fold_in(jax.random.fold_in(rng, 6), axis_at), (shards_of,), jnp.float32, smallest / len(cuts), top_value / len(cuts))
        return jnp.repeat(jnp.exp(draws), dims[axis_at] // shards_of).reshape((-1,) + (1,) * (len(dims) - axis_at - 1))

    level = one(*cuts[0])
    for cut in cuts[1:]:
        level = level * one(*cut)
    return level


def noise(stream_key, shape, width, bound, cuts=(), kind=jnp.bfloat16):
    values = width * jax.random.normal(stream_key, shape, jnp.float32)
    if cuts:
        values = values * level_of(stream_key, shape, cuts, -0.22, 0.18)
    return jnp.clip(values, -bound, bound).astype(kind)


def setup_inputs(seed: int = 0) -> dict:
    key_of = jax.random.split(jax.random.key(seed), 7)
    return {
        "starts": noise(key_of[0], (TIME_SLABS, GRID_SUBNETWORKS, GRID_NODES, CASES), 1.0, 6.0, ((0, 32), (1, 4)), jnp.float32),
        "sources": noise(key_of[1], (TIME_SLABS, GRID_SUBNETWORKS, GRID_NODES, CASES), 1.0, 6.0, ((0, 32), (1, 4))),
        "inverse_conductance": draw_inverse_conductance(jax.random.fold_in(key_of[6], 71), 0),
        "coarse_decay": draw_coarse_decay(jax.random.fold_in(key_of[6], 71), 0),
        "interface_nodes": draw_interface_nodes(jax.random.fold_in(key_of[6], 71), 0),
        "retire": draw_retire(jax.random.fold_in(key_of[6], 71), 0),
    }


def fine_slab(start, source, inverse_conductance, interface_nodes):
    state = start
    source_f = source.astype(jnp.float32)
    for step in range(STEPS):
        stepped = (state + source_f).astype(jnp.bfloat16)
        products = jnp.stack([jnp.dot(inverse_conductance[s], stepped[s], preferred_element_type=jnp.float32) for s in range(GRID_SUBNETWORKS)])
        rows = jax.vmap(lambda block, where_at: block[where_at])(products, interface_nodes)
        mean_iface = jnp.sum(rows, axis=0) / GRID_SUBNETWORKS
        state = jax.vmap(lambda block, where_at: block.at[where_at].set(mean_iface))(products, interface_nodes)
    return state


def reference(starts, sources, inverse_conductance, coarse_decay, interface_nodes, retire):
    fine = lax.map(lambda pair: fine_slab(pair[0], pair[1], inverse_conductance, interface_nodes), (starts, sources))
    correction = fine - coarse_decay[..., None] * starts

    def advance(state, inputs):
        decay_n, corr_n = inputs
        return decay_n[..., None] * state + corr_n, state

    last, states = lax.scan(advance, starts[0], (coarse_decay, correction))
    every = jnp.concatenate([states, last[None]], axis=0)
    position = jnp.arange(TIME_SLABS, dtype=jnp.int32)[:, None] + retire[None, :]
    position = jnp.minimum(position, TIME_SLABS).astype(jnp.int32)
    index = jnp.broadcast_to(position[:, None, None, :], (TIME_SLABS, GRID_SUBNETWORKS, GRID_NODES, CASES))
    return jnp.take_along_axis(every, index, axis=0)
```

```python
import functools

import jax
import jax.numpy as jnp
from jax import lax
from jax.experimental import pallas as pl
from jax.experimental.pallas import tpu as pltpu
from jax.sharding import PartitionSpec as P

NODES = 2048
CASES = 128
IFACE = 256
STEPS = 8
SUBS = 8
SLABS = 32
CHIPS = SLABS // 2
PIECE = NODES // CHIPS
HALF = IFACE // 2
MESH = pl.DeviceIdType.MESH
F32, BF16 = jnp.float32, jnp.bfloat16


def dot(a, b):
    return jnp.dot(a, b, preferred_element_type=F32)


def split2(value):
    high = value.astype(BF16)
    return high, (value - high.astype(F32)).astype(BF16)


def block(index, size):
    return pl.ds(pl.multiple_of(index * size, size), size)


def column(row):
    return jnp.broadcast_to(row, (128, 128)).T


def kernel(
    dec_ref, idxc_ref, idxr_ref, ret_ref, starts_ref, sources_ref, cond_ref,
    out_ref,
    a, e, et, ai, ac, w, z, src, st, sbo, sbx, sf, rf, mask, dcol, dpk, decall,
    sI, bq, kh, kl, km, mh, ml, wI, tot,
    q, ra, h, rb, hb, rc, ss, rd,
    cc, cs, inbox, outbox, yb, c2, ws, rw, ob,
    lsem, asem, swsem, swrec, dsend, drecv,
    as_, ar_, bs_, br_, cs_, cr_, ds_, dr_,
    tis, tir, tos, tor, shs, shr, ws_, wr_,
):
    s, u = lax.axis_index("slab"), lax.axis_index("sub")
    c = lax.rem(s, 2)
    m = lax.div(s, 2)
    oc = 1 - c
    mate = (s + 1 - 2 * c, u)
    first = (s, u + 1 - 2 * lax.rem(u, 2))
    second = (s, 3 - u)

    loads = [
        pltpu.make_async_copy(cond_ref.at[c, pl.ds(i * 512, 512)], a.at[pl.ds(i * 512, 512)], asem.at[i])
        for i in range(4)
    ]
    load_sbx = pltpu.make_async_copy(sources_ref.at[oc], sbx, lsem.at[0])
    load_sbo = pltpu.make_async_copy(sources_ref.at[c], sbo, lsem.at[1])
    load_st = pltpu.make_async_copy(starts_ref.at[c], st.at[c], lsem.at[2])
    load_sbx.start()
    for load in loads:
        load.start()
    load_sbo.start()
    load_st.start()

    barrier = pltpu.get_barrier_semaphore()

    def greet(j, _):
        pl.semaphore_signal(barrier, inc=1, device_id=(lax.rem(s + j, SLABS), u), device_id_type=MESH)
        return 0

    lax.fori_loop(1, SLABS, greet, 0)
    pl.semaphore_signal(barrier, inc=1, device_id=first, device_id_type=MESH)
    pl.semaphore_signal(barrier, inc=1, device_id=second, device_id_type=MESH)
    pl.semaphore_wait(barrier, SLABS + 1)

    def remote(source, target, send, receive, to):
        return pltpu.make_async_remote_copy(
            src_ref=source, dst_ref=target, send_sem=send, recv_sem=receive,
            device_id=to, device_id_type=MESH,
        )

    swap_st = remote(starts_ref.at[oc], st.at[c], swsem.at[0], swrec.at[0], mate)
    swap_st.start()
    load_sbx.wait()
    sf[...] = sbx[...].astype(F32)
    swap_src = remote(sf, rf, swsem.at[1], swrec.at[1], mate)
    swap_src.start()

    def decay_out(j):
        t = lax.rem(s + j, SLABS)
        return remote(dec_ref.at[lax.rem(t, 2)], decall.at[s], dsend.at[j], drecv.at[s], (t, u))

    def decay_in(j):
        t = lax.rem(s + j, SLABS)
        return remote(dec_ref.at[c], decall.at[t], dsend.at[j], drecv.at[t], (t, u))

    def go(make):
        def one(j, _):
            make(j).start()
            return 0
        return one

    lax.fori_loop(1, SLABS, go(decay_out), 0)
    decall[s] = dec_ref[c]

    e[...] = (lax.broadcasted_iota(jnp.int32, (IFACE, NODES), 1) == idxc_ref[c]).astype(F32).astype(BF16)
    et[...] = (lax.broadcasted_iota(jnp.int32, (NODES, IFACE), 0) == idxr_ref[c]).astype(F32).astype(BF16)
    for load in loads:
        load.wait()

    def rows_of_interface(i, _):
        ai[:, block(i, 512)] = dot(e[...], a[:, block(i, 512)]).astype(BF16)
        return 0

    lax.fori_loop(0, 4, rows_of_interface, 0)
    aii = dot(ai[...], et[...])
    q[0, 0] = aii[:, :CASES]
    q[0, 1] = aii[:, CASES:]

    def ex_a(p):
        return remote(q.at[p, oc], ra.at[p], as_.at[p], ar_.at[p], mate)

    def ex_b(p):
        return [
            remote(h.at[p, pl.ds(0, HALF)], rb.at[p, pl.ds(0, HALF)], bs_.at[p, 0], br_.at[p, 0], first),
            remote(h.at[p, pl.ds(HALF, HALF)], rb.at[p, pl.ds(HALF, HALF)], bs_.at[p, 1], br_.at[p, 1], second),
        ]

    def ex_c(p):
        return [
            remote(hb.at[p, pl.ds(0, HALF)], rc.at[p, pl.ds(0, HALF)], cs_.at[p, 0], cr_.at[p, 0], second),
            remote(hb.at[p, pl.ds(HALF, HALF)], rc.at[p, pl.ds(HALF, HALF)], cs_.at[p, 1], cr_.at[p, 1], first),
        ]

    def ex_d(p):
        return remote(ss.at[p], rd.at[p], ds_.at[p], dr_.at[p], mate)

    def a_to_b(p):
        ex_a(p).wait()
        h[p] = q[p, c] + ra[p]
        for copy in ex_b(p):
            copy.start()

    def b_to_c(p):
        for copy in ex_b(p):
            copy.wait()
        hb[p] = h[p] + rb[p]
        for copy in ex_c(p):
            copy.start()

    def c_to_d(p):
        for copy in ex_c(p):
            copy.wait()
        ss[p] = hb[p] + rc[p]
        ex_d(p).start()

    def d_done(p):
        ex_d(p).wait()
        tot[c] = ss[p]
        tot[oc] = rd[p]

    ex_a(0).start()

    mask[...] = 1.0 - dot(et[...], jnp.ones((IFACE, CASES), BF16))
    a_to_b(0)

    def columns_of_interface(i, _):
        ac[block(i, 512), :] = dot(a[block(i, 512), :], et[...]).astype(BF16)
        return 0

    lax.fori_loop(0, 4, columns_of_interface, 0)

    load_sbo.wait()
    load_st.wait()
    swap_st.wait()
    swap_src.wait()
    src[c] = sbo[...]
    src[oc] = rf[...].astype(BF16)
    for j in range(2):
        w[0, :, j * CASES:(j + 1) * CASES] = (st[j] + src[j].astype(F32)).astype(BF16)
        sI[:, j * CASES:(j + 1) * CASES] = dot(e[...], src[j])
    bq[...] = dot(aii.astype(BF16), sI[...].astype(BF16))
    for ref in (kh, kl, mh, ml, wI):
        ref[...] = jnp.zeros_like(ref)

    def decay_wait(j, _):
        decay_out(j).wait_send()
        decay_in(j).wait_recv()
        return 0

    lax.fori_loop(1, SLABS, decay_wait, 0)
    b_to_c(0)

    def advance_mean():
        return km[...] + jnp.concatenate([tot[0], tot[1]], axis=1) * (1.0 / SUBS)

    def carry_mean():
        km[...] = dot(kh[...], mh[...]) + dot(kh[...], ml[...]) + dot(kl[...], mh[...])

    after = jnp.minimum(2 * m + 2, SLABS - 1)

    def step(k, _):
        p, pn = lax.rem(k, 2), lax.rem(k + 1, 2)
        qv = dot(ai[...], w[p]) + jnp.where(k > 0, 1.0, 0.0) * bq[...]
        q[pn, 0] = qv[:, :CASES]
        q[pn, 1] = qv[:, CASES:]
        ex_a(pn).start()
        carry_mean()
        for i in range(2):
            z[i * 512:(i + 1) * 512, :] = dot(a[i * 512:(i + 1) * 512, :], w[p])
        a_to_b(pn)
        for i in range(2):
            b = 2 * k + i
            dcol[0, block(b, 128), :] = column(decall[2 * m, pl.ds(b, 1), :])
            dcol[1, block(b, 128), :] = column(decall[2 * m + 1, pl.ds(b, 1), :])
            dcol[2, block(b, 128), :] = column(decall[after, pl.ds(b, 1), :])
            dpk[b] = column(decall[2 * b, pl.ds(m, 1), :] * decall[2 * b + 1, pl.ds(m, 1), :])
        c_to_d(p)
        for i in range(2, 4):
            z[i * 512:(i + 1) * 512, :] = dot(a[i * 512:(i + 1) * 512, :], w[p])
        d_done(p)

        @pl.when(k == 0)
        def _():
            high, low = split2(advance_mean())
            kh[...] = high
            kl[...] = low

        @pl.when(k > 0)
        def _():
            mean = advance_mean()
            high, low = split2(mean)
            mh[...] = high
            ml[...] = low
            wI[...] = (mean + sI[...]).astype(BF16)

        for i in range(4):
            rows = slice(i * 512, (i + 1) * 512)
            zf = z[rows, :] + dot(ac[rows, :], wI[...])
            z[rows, :] = zf
            for j in range(2):
                lanes = slice(j * CASES, (j + 1) * CASES)
                w[pn, rows, lanes] = (mask[rows, :] * (zf[:, lanes] + src[j, rows, :].astype(F32))).astype(BF16)
        b_to_c(pn)
        return 0

    lax.fori_loop(0, STEPS, step, 0)

    carry_mean()
    c_to_d(0)
    d_done(0)
    mean = advance_mean()
    m1, rest = mean.astype(BF16), mean - mean.astype(BF16).astype(F32)
    m2, m3 = split2(rest)
    kh[...] = m1
    kl[...] = m2
    mh[...] = m3

    def corrections(i, _):
        rows = block(i, 256)
        spread = dot(et[rows, :], kh[...]) + dot(et[rows, :], kl[...]) + dot(et[rows, :], mh[...])
        f0 = z[rows, :CASES] * mask[rows, :] + spread[:, :CASES]
        f1 = z[rows, CASES:] * mask[rows, :] + spread[:, CASES:]
        c0 = f0 - dcol[0, rows, :] * st[0, rows, :]
        c1 = f1 - dcol[1, rows, :] * st[1, rows, :]
        cc[0, rows, :] = c0
        cc[1, rows, :] = c1
        cs[rows, :] = dcol[1, rows, :] * jnp.where(m == 0, f0, c0) + c1
        return 0

    lax.fori_loop(0, NODES // 256, corrections, 0)

    def to_chip(o):
        t = lax.rem(m + o, CHIPS)
        return t, (2 * t + c, u)

    def in_out(o):
        t, there = to_chip(o)
        return remote(cs.at[block(t, PIECE)], inbox.at[m], tis.at[o], tir.at[m], there)

    def in_in(o):
        t, there = to_chip(o)
        return remote(cs.at[block(t, PIECE)], inbox.at[t], tis.at[o], tir.at[t], there)

    lax.fori_loop(1, CHIPS, go(in_out), 0)
    back = lax.rem(m + CHIPS - 1, CHIPS)
    shift = remote(cc.at[0], c2, shs, shr, (2 * back + c, u))
    shift.start()
    inbox[m] = cs[block(m, PIECE), :]

    def in_wait(o, _):
        in_out(o).wait_send()
        in_in(o).wait_recv()
        return 0

    lax.fori_loop(1, CHIPS, in_wait, 0)

    retire = ret_ref[...]

    def scan(k, state):
        new = dpk[k] * state + inbox[k]
        outbox[k] = jnp.where(retire >= 2, new, state)
        return new

    lax.fori_loop(0, CHIPS, scan, jnp.zeros((PIECE, CASES), F32))

    def back_out(o):
        t, there = to_chip(o)
        return remote(outbox.at[t], yb.at[block(m, PIECE)], tos.at[o], tor.at[m], there)

    def back_in(o):
        t, there = to_chip(o)
        return remote(outbox.at[t], yb.at[block(t, PIECE)], tos.at[o], tor.at[t], there)

    lax.fori_loop(1, CHIPS, go(back_out), 0)
    yb[block(m, PIECE), :] = outbox[m]
    shift.wait()

    def to_mate(j):
        rows = block(j, PIECE)
        return remote(ws.at[rows], rw.at[rows], ws_.at[j], wr_.at[j], mate)

    last = m == CHIPS - 1

    def finish(j):
        rows = block(j, PIECE)
        got = yb[rows, :]
        zero = jnp.logical_and(m == 0, retire < 2)
        got = jnp.where(zero, st[0, rows, :], got)
        v1 = dcol[0, rows, :] * got + cc[0, rows, :]
        v2 = dcol[1, rows, :] * v1 + cc[1, rows, :]
        v3 = jnp.where(last, got, dcol[2, rows, :] * got + c2[rows, :])
        w0 = jnp.where(retire == 1, v1, got)
        w1 = jnp.where(retire == 0, v1, jnp.where(retire == 1, v2, v3))
        ob[rows, :] = jnp.where(c == 0, w0, w1)
        ws[rows, :] = jnp.where(c == 0, w1, w0)
        to_mate(j).start()

    finish(m)

    def finish_at(o, _):
        t = lax.rem(m + CHIPS - o, CHIPS)
        back_in(CHIPS - o).wait_recv()
        finish(t)
        return 0

    lax.fori_loop(1, CHIPS, finish_at, 0)
    store_own = pltpu.make_async_copy(ob, out_ref.at[c], lsem.at[0])
    store_own.start()

    def last_waits(j, _):
        to_mate(j).wait()
        return 0

    lax.fori_loop(0, CHIPS, last_waits, 0)
    store_other = pltpu.make_async_copy(rw, out_ref.at[oc], lsem.at[1])
    store_other.start()

    def back_sent(o, _):
        back_out(o).wait_send()
        return 0

    lax.fori_loop(1, CHIPS, back_sent, 0)
    store_own.wait()
    store_other.wait()


def body(starts, sources, inverse_conductance, coarse_decay, interface_nodes, retire):
    hbm = pl.BlockSpec(memory_space=pl.ANY)
    vmem = pl.BlockSpec(memory_space=pltpu.VMEM)
    V, D = pltpu.VMEM, pltpu.SemaphoreType.DMA
    whole = (NODES, CASES)
    wide = (NODES, 2 * CASES)
    ifw = (IFACE, 2 * CASES)
    ex = (2, IFACE, CASES)
    scratch = [
        V((NODES, NODES), BF16), V((IFACE, NODES), BF16), V((NODES, IFACE), BF16),
        V((IFACE, NODES), BF16), V((NODES, IFACE), BF16),
        V((2,) + wide, BF16), V(wide, F32), V((2,) + whole, BF16), V((2,) + whole, F32),
        V(whole, BF16), V(whole, BF16), V(whole, F32), V(whole, F32), V(whole, F32),
        V((3,) + whole, F32), V((CHIPS, PIECE, CASES), F32), V((SLABS, 16, 128), F32),
        V(ifw, F32), V(ifw, F32), V((IFACE, IFACE), BF16), V((IFACE, IFACE), BF16), V(ifw, F32),
        V(ifw, BF16), V(ifw, BF16), V(ifw, BF16), V(ex, F32),
        V((2,) + ex, F32), V(ex, F32), V(ex, F32), V(ex, F32), V(ex, F32), V(ex, F32), V(ex, F32), V(ex, F32),
        V((2,) + whole, F32), V(whole, F32), V((CHIPS, PIECE, CASES), F32), V((CHIPS, PIECE, CASES), F32),
        V(whole, F32), V(whole, F32), V(whole, F32), V(whole, F32), V(whole, F32),
        D((3,)), D((4,)), D((2,)), D((2,)), D((SLABS,)), D((SLABS,)),
        D((2,)), D((2,)), D((2, 2)), D((2, 2)), D((2, 2)), D((2, 2)), D((2,)), D((2,)),
        D((CHIPS,)), D((CHIPS,)), D((CHIPS,)), D((CHIPS,)), D, D, D((CHIPS,)), D((CHIPS,)),
    ]
    out = pl.pallas_call(
        kernel,
        out_shape=jax.ShapeDtypeStruct((2,) + whole, F32),
        in_specs=[vmem] * 4 + [hbm] * 3,
        out_specs=hbm,
        scratch_shapes=scratch,
        compiler_params=pltpu.CompilerParams(
            collective_id=0, has_side_effects=True, vmem_limit_bytes=56 << 20
        ),
        cost_estimate=pl.CostEstimate(flops=2 * 9 * 2304 * 2304 * 256, bytes_accessed=16 << 20, transcendentals=0),
        name="parareal",
    )(
        coarse_decay.reshape(2, 16, 128),
        interface_nodes.reshape(2, IFACE, 1),
        interface_nodes.reshape(2, 1, IFACE),
        retire.reshape(1, CASES),
        starts[0],
        sources[0],
        inverse_conductance,
    )
    return out[None]


def solution(mesh):
    return jax.shard_map(
        body,
        mesh=mesh,
        in_specs=(
            P("slab", "sub", None, None),
            P("slab", "sub", None, None),
            P("sub", None, None),
            P("slab", "sub", None),
            P("sub", None),
            P(),
        ),
        out_specs=P("slab", "sub", None, None),
        check_vma=False,
    )
```

```python
import functools

import jax
import jax.numpy as jnp
from jax import lax
from jax.experimental import pallas as pl
from jax.experimental.pallas import tpu as pltpu
from jax.sharding import PartitionSpec as P

NODES = 2048
CASES = 128
IFACE = 256
STEPS = 8
SUBS = 8
SLABS = 32
CHIPS = SLABS // 2
PIECE = NODES // CHIPS
HALF = IFACE // 2
EARLY = 6
SLOTS = 3
MESH = pl.DeviceIdType.MESH
F32, BF16 = jnp.float32, jnp.bfloat16


def dot(a, b):
    return jnp.dot(a, b, preferred_element_type=F32)


def split2(value):
    high = value.astype(BF16)
    return high, (value - high.astype(F32)).astype(BF16)


def block(index, size):
    return pl.ds(pl.multiple_of(index * size, size), size)


def column(row):
    return jnp.broadcast_to(row, (128, 128)).T


def kernel(
    decay_ref, idx_ref, ret_ref, starts_ref, sources_ref, cond_ref,
    out_ref,
    dec_ref, a, e, et, ai, ac, w, z, src, st, sbo, sbx, sf, rf, mask, dcol, dpk, decall,
    sI, bq, gc, sg, k0h, k0l, k1h, k1l, m1h, m1l, m2h, m2l, tot,
    q, ra, h, rb, hb, rc, ss, rd,
    cc, cs, inbox, outbox, yb, c2, ws, rw, ob,
    lsem, asem, swsem, swrec, dsend, drecv,
    as_, ar_, bs_, br_, cs_, cr_, ds_, dr_,
    tis, tir, tos, tor, shs, shr, ws_, wr_,
):
    s, u = lax.axis_index("slab"), lax.axis_index("sub")
    c = lax.rem(s, 2)
    m = lax.div(s, 2)
    oc = 1 - c
    mate = (s + 1 - 2 * c, u)
    first = (s, u + 1 - 2 * lax.rem(u, 2))
    second = (s, 3 - u)

    loads = [
        pltpu.make_async_copy(cond_ref.at[c, pl.ds(i * 512, 512)], a.at[pl.ds(i * 512, 512)], asem.at[i])
        for i in range(4)
    ]
    load_sbx = pltpu.make_async_copy(sources_ref.at[oc], sbx, lsem.at[0])
    load_sbo = pltpu.make_async_copy(sources_ref.at[c], sbo, lsem.at[1])
    load_st = pltpu.make_async_copy(starts_ref.at[c], st.at[c], lsem.at[2])
    load_sbx.start()
    for load in loads:
        load.start()
    load_sbo.start()
    load_st.start()

    barrier = pltpu.get_barrier_semaphore()

    def greet(j, _):
        pl.semaphore_signal(barrier, inc=1, device_id=(lax.rem(s + j, SLABS), u), device_id_type=MESH)
        return 0

    lax.fori_loop(1, SLABS, greet, 0)
    pl.semaphore_signal(barrier, inc=1, device_id=first, device_id_type=MESH)
    pl.semaphore_signal(barrier, inc=1, device_id=second, device_id_type=MESH)

    for j in range(2):
        for b in range(16):
            dec_ref[j, b:b + 1, :] = decay_ref[j:j + 1, b * 128:(b + 1) * 128]
    nodes_at = idx_ref[pl.ds(c, 1), :].astype(F32)
    et[...] = (lax.broadcasted_iota(jnp.int32, (NODES, IFACE), 0).astype(F32) == nodes_at).astype(F32).astype(BF16)
    lane = lax.broadcasted_iota(jnp.int32, (128, 128), 1).astype(F32)
    for i in range(2):
        nodes_down = column(nodes_at[:, i * 128:(i + 1) * 128])
        for b in range(16):
            e[i * 128:(i + 1) * 128, b * 128:(b + 1) * 128] = (lane + float(b * 128) == nodes_down).astype(F32).astype(BF16)
    pl.semaphore_wait(barrier, SLABS + 1)

    def remote(source, target, send, receive, to):
        return pltpu.make_async_remote_copy(
            src_ref=source, dst_ref=target, send_sem=send, recv_sem=receive,
            device_id=to, device_id_type=MESH,
        )

    swap_st = remote(starts_ref.at[oc], st.at[c], swsem.at[0], swrec.at[0], mate)
    swap_st.start()
    load_sbx.wait()
    sf[...] = sbx[...].astype(F32)
    swap_src = remote(sf, rf, swsem.at[1], swrec.at[1], mate)
    swap_src.start()

    def decay_out(j):
        t = lax.rem(s + j, SLABS)
        return remote(dec_ref.at[lax.rem(t, 2)], decall.at[s], dsend.at[j], drecv.at[s], (t, u))

    def decay_in(j):
        t = lax.rem(s + j, SLABS)
        return remote(dec_ref.at[c], decall.at[t], dsend.at[j], drecv.at[t], (t, u))

    def go(make):
        def one(j, _):
            make(j).start()
            return 0
        return one

    lax.fori_loop(1, SLABS, go(decay_out), 0)
    decall[s] = dec_ref[c]

    for load in loads:
        load.wait()

    def rows_of_interface(i, _):
        ai[:, block(i, 512)] = dot(e[...], a[:, block(i, 512)]).astype(BF16)
        return 0

    lax.fori_loop(0, 4, rows_of_interface, 0)
    aii = dot(ai[...], et[...])
    q[0, 0] = aii[:, :CASES]
    q[0, 1] = aii[:, CASES:]

    def ex_a(p):
        return remote(q.at[p, oc], ra.at[p], as_.at[p], ar_.at[p], mate)

    def ex_b(p):
        return [
            remote(h.at[p, pl.ds(0, HALF)], rb.at[p, pl.ds(0, HALF)], bs_.at[p, 0], br_.at[p, 0], first),
            remote(h.at[p, pl.ds(HALF, HALF)], rb.at[p, pl.ds(HALF, HALF)], bs_.at[p, 1], br_.at[p, 1], second),
        ]

    def ex_c(p):
        return [
            remote(hb.at[p, pl.ds(0, HALF)], rc.at[p, pl.ds(0, HALF)], cs_.at[p, 0], cr_.at[p, 0], second),
            remote(hb.at[p, pl.ds(HALF, HALF)], rc.at[p, pl.ds(HALF, HALF)], cs_.at[p, 1], cr_.at[p, 1], first),
        ]

    def ex_d(p):
        return remote(ss.at[p], rd.at[p], ds_.at[p], dr_.at[p], mate)

    def a_to_b(p):
        ex_a(p).wait()
        h[p] = q[p, c] + ra[p]
        for copy in ex_b(p):
            copy.start()

    def b_to_c(p):
        for copy in ex_b(p):
            copy.wait()
        hb[p] = h[p] + rb[p]
        for copy in ex_c(p):
            copy.start()

    def c_to_d(p):
        for copy in ex_c(p):
            copy.wait()
        ss[p] = hb[p] + rc[p]
        ex_d(p).start()

    def d_done(p):
        ex_d(p).wait()
        tot[c] = ss[p]
        tot[oc] = rd[p]

    ex_a(0).start()

    mask[...] = 1.0 - dot(et[...], jnp.ones((IFACE, CASES), BF16))

    def columns_of_interface(i, _):
        rows = block(i, 512)
        columns = dot(a[rows, :], et[...])
        ac[rows, :] = columns.astype(BF16)
        for j in range(2):
            lanes = slice(j * CASES, (j + 1) * CASES)
            w[1, rows, lanes] = (columns[:, lanes] * mask[rows, :]).astype(BF16)
        return 0

    lax.fori_loop(0, 4, columns_of_interface, 0)
    a_to_b(0)
    kv = dot(ai[...], w[1])
    q[1, 0] = kv[:, :CASES]
    q[1, 1] = kv[:, CASES:]
    ex_a(1).start()

    def columns_twice(i, _):
        rows = block(i, 512)
        gc[rows, :] = dot(a[rows, :], w[1]).astype(BF16)
        return 0

    lax.fori_loop(0, 4, columns_twice, 0)
    a_to_b(1)

    load_sbo.wait()
    load_st.wait()
    swap_st.wait()
    swap_src.wait()
    src[c] = sbo[...]
    src[oc] = rf[...].astype(BF16)
    for j in range(2):
        w[0, :, j * CASES:(j + 1) * CASES] = (st[j] + src[j].astype(F32)).astype(BF16)
        sI[:, j * CASES:(j + 1) * CASES] = dot(e[...], src[j])
    bq[...] = dot(aii.astype(BF16), sI[...].astype(BF16))

    def constant_source(i, _):
        rows = block(i, 512)
        fixed = dot(ac[rows, :], sI[...].astype(BF16))
        for j in range(2):
            lanes = slice(j * CASES, (j + 1) * CASES)
            sg[j, rows, :] = fixed[:, lanes]
        return 0

    lax.fori_loop(0, 4, constant_source, 0)
    for ref in (k0h, k0l, k1h, k1l, m1h, m1l, m2h, m2l):
        ref[...] = jnp.zeros_like(ref)

    def decay_wait(j, _):
        decay_out(j).wait_send()
        decay_in(j).wait_recv()
        return 0

    lax.fori_loop(1, SLABS, decay_wait, 0)
    b_to_c(0)

    def total():
        return jnp.concatenate([tot[0], tot[1]], axis=1) * (1.0 / SUBS)

    def next_mean():
        mean = dot(k0h[...], m1h[...]) + dot(k0h[...], m1l[...]) + dot(k0l[...], m1h[...])
        mean += dot(k1h[...], m2h[...]) + dot(k1h[...], m2l[...]) + dot(k1l[...], m2h[...])
        return mean + total()

    def push_mean():
        mean = next_mean()
        m2h[...] = m1h[...]
        m2l[...] = m1l[...]
        high, low = split2(mean)
        m1h[...] = high
        m1l[...] = low
        return mean

    after = jnp.minimum(2 * m + 2, SLABS - 1)

    def step(k, _):
        p, pn = lax.rem(k, 2), lax.rem(k + 1, 2)
        now, next1, next2 = lax.rem(k, SLOTS), lax.rem(k + 1, SLOTS), lax.rem(k + 2, SLOTS)
        later = jnp.where(k > 0, 1.0, 0.0)
        qv = dot(ai[...], w[p]) + later * bq[...]
        q[next2, 0] = qv[:, :CASES]
        q[next2, 1] = qv[:, CASES:]
        ex_a(next2).start()
        def part(i):
            z[i * 512:(i + 1) * 512, :] = dot(a[i * 512:(i + 1) * 512, :], w[p])

        part(0)
        part(1)
        a_to_b(next2)
        b_to_c(next1)
        c_to_d(now)
        part(2)
        for i in range(2):
            b = 2 * k + i
            dcol[0, block(b, 128), :] = column(decall[2 * m, pl.ds(b, 1), :])
            dcol[1, block(b, 128), :] = column(decall[2 * m + 1, pl.ds(b, 1), :])
            dcol[2, block(b, 128), :] = column(decall[after, pl.ds(b, 1), :])
            dpk[b] = column(decall[2 * b, pl.ds(m, 1), :] * decall[2 * b + 1, pl.ds(m, 1), :])
        part(3)
        d_done(now)

        @pl.when(k == 0)
        def _():
            high, low = split2(total())
            k0h[...] = high
            k0l[...] = low

        @pl.when(k == 1)
        def _():
            high, low = split2(total())
            k1h[...] = high
            k1l[...] = low

        @pl.when(k > 1)
        def _():
            push_mean()

        for i in range(4):
            rows = slice(i * 512, (i + 1) * 512)
            more = dot(gc[rows, :], m1h[...])
            for j in range(2):
                lanes = slice(j * CASES, (j + 1) * CASES)
                zf = z[rows, lanes] + more[:, lanes] + later * sg[j, rows, :]
                z[rows, lanes] = zf
                w[pn, rows, lanes] = (mask[rows, :] * (zf + src[j, rows, :].astype(F32))).astype(BF16)
        return 0

    lax.fori_loop(0, STEPS, step, 0)

    now, next1 = STEPS % SLOTS, (STEPS + 1) % SLOTS
    c_to_d(now)
    b_to_c(next1)
    d_done(now)
    push_mean()

    def last_columns(i, _):
        rows = block(i, 512)
        z[rows, :] += dot(ac[rows, :], m1h[...])
        return 0

    lax.fori_loop(0, 4, last_columns, 0)
    c_to_d(next1)
    d_done(next1)
    mean = next_mean()
    p1, rest = mean.astype(BF16), mean - mean.astype(BF16).astype(F32)
    p2, p3 = split2(rest)
    k0h[...] = p1
    k0l[...] = p2
    k1h[...] = p3

    def to_chip(o):
        t = lax.rem(m + o, CHIPS)
        return t, (2 * t + c, u)

    def in_out(o):
        t, there = to_chip(o)
        return remote(cs.at[block(t, PIECE)], inbox.at[m], tis.at[o], tir.at[m], there)

    def in_in(o):
        t, there = to_chip(o)
        return remote(cs.at[block(t, PIECE)], inbox.at[t], tis.at[o], tir.at[t], there)

    back = lax.rem(m + CHIPS - 1, CHIPS)

    def shift(t):
        rows = block(t, PIECE)
        return remote(cc.at[0, rows], c2.at[rows], shs.at[t], shr.at[t], (2 * back + c, u))

    def corrections(o, _):
        t = lax.rem(m + o, CHIPS)
        rows = block(t, PIECE)
        spread = dot(et[rows, :], k0h[...]) + dot(et[rows, :], k0l[...]) + dot(et[rows, :], k1h[...])
        f0 = z[rows, :CASES] * mask[rows, :] + spread[:, :CASES]
        f1 = z[rows, CASES:] * mask[rows, :] + spread[:, CASES:]
        c0 = f0 - dcol[0, rows, :] * st[0, rows, :]
        c1 = f1 - dcol[1, rows, :] * st[1, rows, :]
        cc[0, rows, :] = c0
        cc[1, rows, :] = c1
        cs[rows, :] = dcol[1, rows, :] * jnp.where(m == 0, f0, c0) + c1

        @pl.when(o < CHIPS)
        def _():
            in_out(o).start()

        @pl.when(jnp.logical_or(o <= EARLY, o == CHIPS))
        def _():
            shift(t).start()

        return 0

    lax.fori_loop(1, CHIPS + 1, corrections, 0)
    inbox[m] = cs[block(m, PIECE), :]

    def in_wait(o, _):
        in_out(o).wait_send()
        in_in(o).wait_recv()
        return 0

    lax.fori_loop(1, CHIPS, in_wait, 0)

    retire = ret_ref[...]

    def scan(k, state):
        new = dpk[k] * state + inbox[k]
        outbox[k] = jnp.where(retire >= 2, new, state)
        return new

    lax.fori_loop(0, CHIPS, scan, jnp.zeros((PIECE, CASES), F32))

    def back_out(o):
        t, there = to_chip(o)
        return remote(outbox.at[t], yb.at[block(m, PIECE)], tos.at[o], tor.at[m], there)

    def back_in(o):
        t, there = to_chip(o)
        return remote(outbox.at[t], yb.at[block(t, PIECE)], tos.at[o], tor.at[t], there)

    def back_go(o, _):
        back_out(o).start()

        @pl.when(o < CHIPS - EARLY)
        def _():
            shift(lax.rem(m + CHIPS - o, CHIPS)).start()

        return 0

    lax.fori_loop(1, CHIPS, back_go, 0)
    yb[block(m, PIECE), :] = outbox[m]

    def to_mate(j):
        rows = block(j, PIECE)
        return remote(ws.at[rows], rw.at[rows], ws_.at[j], wr_.at[j], mate)

    last = m == CHIPS - 1

    def finish(j):
        rows = block(j, PIECE)
        shift(j).wait_recv()
        got = yb[rows, :]
        zero = jnp.logical_and(m == 0, retire < 2)
        got = jnp.where(zero, st[0, rows, :], got)
        v1 = dcol[0, rows, :] * got + cc[0, rows, :]
        v2 = dcol[1, rows, :] * v1 + cc[1, rows, :]
        v3 = jnp.where(last, got, dcol[2, rows, :] * got + c2[rows, :])
        w0 = jnp.where(retire == 1, v1, got)
        w1 = jnp.where(retire == 0, v1, jnp.where(retire == 1, v2, v3))
        ob[rows, :] = jnp.where(c == 0, w0, w1)
        ws[rows, :] = jnp.where(c == 0, w1, w0)
        to_mate(j).start()

    finish(m)

    def finish_at(o, _):
        t = lax.rem(m + CHIPS - o, CHIPS)
        back_in(CHIPS - o).wait_recv()
        finish(t)
        return 0

    lax.fori_loop(1, CHIPS, finish_at, 0)
    store_own = pltpu.make_async_copy(ob, out_ref.at[c], lsem.at[0])
    store_own.start()

    def last_waits(j, _):
        to_mate(j).wait()
        shift(j).wait_send()
        return 0

    lax.fori_loop(0, CHIPS, last_waits, 0)
    store_other = pltpu.make_async_copy(rw, out_ref.at[oc], lsem.at[1])
    store_other.start()

    def back_sent(o, _):
        back_out(o).wait_send()
        return 0

    lax.fori_loop(1, CHIPS, back_sent, 0)
    store_own.wait()
    store_other.wait()


def body(starts, sources, inverse_conductance, coarse_decay, interface_nodes, retire):
    hbm = pl.BlockSpec(memory_space=pl.ANY)
    vmem = pl.BlockSpec(memory_space=pltpu.VMEM)
    V, D = pltpu.VMEM, pltpu.SemaphoreType.DMA
    whole = (NODES, CASES)
    wide = (NODES, 2 * CASES)
    ifw = (IFACE, 2 * CASES)
    ex = (2, IFACE, CASES)
    scratch = [
        V((2, 16, 128), F32), V((NODES, NODES), BF16), V((IFACE, NODES), BF16), V((NODES, IFACE), BF16),
        V((IFACE, NODES), BF16), V((NODES, IFACE), BF16),
        V((2,) + wide, BF16), V(wide, F32), V((2,) + whole, BF16), V((2,) + whole, F32),
        V(whole, BF16), V(whole, BF16), V(whole, F32), V(whole, F32), V(whole, F32),
        V((3,) + whole, F32), V((CHIPS, PIECE, CASES), F32), V((SLABS, 16, 128), F32),
        V(ifw, F32), V(ifw, F32), V((NODES, IFACE), BF16), V((2,) + whole, F32),
        *[V(ifw, BF16)] * 8, V(ex, F32),
        V((SLOTS,) + ex, F32), *[V((SLOTS, IFACE, CASES), F32)] * 7,
        V((2,) + whole, F32), V(whole, F32), V((CHIPS, PIECE, CASES), F32), V((CHIPS, PIECE, CASES), F32),
        V(whole, F32), V(whole, F32), V(whole, F32), V(whole, F32), V(whole, F32),
        D((3,)), D((4,)), D((2,)), D((2,)), D((SLABS,)), D((SLABS,)),
        D((SLOTS,)), D((SLOTS,)), *[D((SLOTS, 2))] * 4, D((SLOTS,)), D((SLOTS,)),
        D((CHIPS,)), D((CHIPS,)), D((CHIPS,)), D((CHIPS,)), D((CHIPS,)), D((CHIPS,)), D((CHIPS,)), D((CHIPS,)),
    ]
    out = pl.pallas_call(
        kernel,
        out_shape=jax.ShapeDtypeStruct((2,) + whole, F32),
        in_specs=[vmem] * 3 + [hbm] * 3,
        out_specs=hbm,
        scratch_shapes=scratch,
        compiler_params=pltpu.CompilerParams(
            collective_id=0, has_side_effects=True, vmem_limit_bytes=56 << 20
        ),
        cost_estimate=pl.CostEstimate(flops=2 * 9 * 2304 * 2304 * 256, bytes_accessed=16 << 20, transcendentals=0),
        name="parareal",
    )(
        coarse_decay[0],
        interface_nodes,
        retire.reshape(1, CASES),
        starts[0],
        sources[0],
        inverse_conductance,
    )
    return out[None]


def solution(mesh):
    return jax.shard_map(
        body,
        mesh=mesh,
        in_specs=(
            P("slab", "sub", None, None),
            P("slab", "sub", None, None),
            P("sub", None, None),
            P("slab", "sub", None),
            P("sub", None),
            P(),
        ),
        out_specs=P("slab", "sub", None, None),
        check_vma=False,
    )
```

```python
import functools

import jax
import jax.numpy as jnp
from jax import lax
from jax.experimental import pallas as pl
from jax.experimental.pallas import tpu as pltpu
from jax.sharding import PartitionSpec as P

NODES = 2048
CASES = 128
IFACE = 256
STEPS = 8
SUBS = 8
SLABS = 32
CHIPS = SLABS // 2
PIECE = NODES // CHIPS
HALF = IFACE // 2
EARLY = 6
SLOTS = 3
MESH = pl.DeviceIdType.MESH
F32, BF16 = jnp.float32, jnp.bfloat16


def dot(a, b):
    return jnp.dot(a, b, preferred_element_type=F32)


def split2(value):
    high = value.astype(BF16)
    return high, (value - high.astype(F32)).astype(BF16)


def block(index, size):
    return pl.ds(pl.multiple_of(index * size, size), size)


def column(row):
    return jnp.broadcast_to(row, (128, 128)).T


def kernel(
    decay_ref, idx_ref, ret_ref, starts_ref, sources_ref, cond_ref,
    out_ref,
    dec_ref, a, e, et, ai, ac, w, z, src, st, sbo, sbx, sf, rf, mask, dcol, dpk, decall,
    sI, bq, gc, sg, k0h, k0l, k1h, k1l, m1h, m1l, m2h, m2l, tot,
    q, ra, h, rb, hb, rc, ss, rd,
    cc, cs, inbox, outbox, yb, c2, ws, rw, ob,
    lsem, asem, swsem, swrec, dsend, drecv,
    as_, ar_, bs_, br_, cs_, cr_, ds_, dr_,
    tis, tir, tos, tor, shs, shr, ws_, wr_,
):
    s, u = lax.axis_index("slab"), lax.axis_index("sub")
    c = lax.rem(s, 2)
    m = lax.div(s, 2)
    oc = 1 - c
    mate = (s + 1 - 2 * c, u)
    first = (s, u + 1 - 2 * lax.rem(u, 2))
    second = (s, 3 - u)

    loads = [
        pltpu.make_async_copy(cond_ref.at[c, pl.ds(i * 512, 512)], a.at[pl.ds(i * 512, 512)], asem.at[i])
        for i in range(4)
    ]
    load_sbx = pltpu.make_async_copy(sources_ref.at[oc], sbx, lsem.at[0])
    load_sbo = pltpu.make_async_copy(sources_ref.at[c], sbo, lsem.at[1])
    load_st = pltpu.make_async_copy(starts_ref.at[c], st.at[c], lsem.at[2])
    load_sbx.start()
    for load in loads:
        load.start()
    load_sbo.start()
    load_st.start()

    barrier = pltpu.get_barrier_semaphore()

    def greet(j, _):
        pl.semaphore_signal(barrier, inc=1, device_id=(lax.rem(s + j, SLABS), u), device_id_type=MESH)
        return 0

    lax.fori_loop(1, SLABS, greet, 0)
    pl.semaphore_signal(barrier, inc=1, device_id=first, device_id_type=MESH)
    pl.semaphore_signal(barrier, inc=1, device_id=second, device_id_type=MESH)

    for j in range(2):
        for b in range(16):
            dec_ref[j, b:b + 1, :] = decay_ref[j:j + 1, b * 128:(b + 1) * 128]
    nodes_at = idx_ref[pl.ds(c, 1), :].astype(F32)
    et[...] = (lax.broadcasted_iota(jnp.int32, (NODES, IFACE), 0).astype(F32) == nodes_at).astype(F32).astype(BF16)
    lane = lax.broadcasted_iota(jnp.int32, (128, 128), 1).astype(F32)
    for i in range(2):
        nodes_down = column(nodes_at[:, i * 128:(i + 1) * 128])
        for b in range(16):
            e[i * 128:(i + 1) * 128, b * 128:(b + 1) * 128] = (lane + float(b * 128) == nodes_down).astype(F32).astype(BF16)

    for load in loads:
        load.wait()
    for i in range(4):
        ai[:, i * 512:(i + 1) * 512] = dot(e[...], a[:, i * 512:(i + 1) * 512]).astype(BF16)
    pl.semaphore_wait(barrier, SLABS + 1)

    def remote(source, target, send, receive, to):
        return pltpu.make_async_remote_copy(
            src_ref=source, dst_ref=target, send_sem=send, recv_sem=receive,
            device_id=to, device_id_type=MESH,
        )

    swap_st = remote(starts_ref.at[oc], st.at[c], swsem.at[0], swrec.at[0], mate)
    swap_st.start()
    load_sbx.wait()
    sf[...] = sbx[...].astype(F32)
    swap_src = remote(sf, rf, swsem.at[1], swrec.at[1], mate)
    swap_src.start()

    def decay_out(j):
        t = lax.rem(s + j, SLABS)
        return remote(dec_ref.at[lax.rem(t, 2)], decall.at[s], dsend.at[j], drecv.at[s], (t, u))

    def decay_in(j):
        t = lax.rem(s + j, SLABS)
        return remote(dec_ref.at[c], decall.at[t], dsend.at[j], drecv.at[t], (t, u))

    def go(make):
        def one(j, _):
            make(j).start()
            return 0
        return one

    lax.fori_loop(1, SLABS, go(decay_out), 0)
    decall[s] = dec_ref[c]

    aii = dot(ai[...], et[...])
    q[0, 0] = aii[:, :CASES]
    q[0, 1] = aii[:, CASES:]

    def ex_a(p):
        return remote(q.at[p, oc], ra.at[p], as_.at[p], ar_.at[p], mate)

    def ex_b(p):
        return [
            remote(h.at[p, pl.ds(0, HALF)], rb.at[p, pl.ds(0, HALF)], bs_.at[p, 0], br_.at[p, 0], first),
            remote(h.at[p, pl.ds(HALF, HALF)], rb.at[p, pl.ds(HALF, HALF)], bs_.at[p, 1], br_.at[p, 1], second),
        ]

    def ex_c(p):
        return [
            remote(hb.at[p, pl.ds(0, HALF)], rc.at[p, pl.ds(0, HALF)], cs_.at[p, 0], cr_.at[p, 0], second),
            remote(hb.at[p, pl.ds(HALF, HALF)], rc.at[p, pl.ds(HALF, HALF)], cs_.at[p, 1], cr_.at[p, 1], first),
        ]

    def ex_d(p):
        return remote(ss.at[p], rd.at[p], ds_.at[p], dr_.at[p], mate)

    def a_to_b(p):
        ex_a(p).wait()
        h[p] = q[p, c] + ra[p]
        for copy in ex_b(p):
            copy.start()

    def b_to_c(p):
        for copy in ex_b(p):
            copy.wait()
        hb[p] = h[p] + rb[p]
        for copy in ex_c(p):
            copy.start()

    def c_to_d(p):
        for copy in ex_c(p):
            copy.wait()
        ss[p] = hb[p] + rc[p]
        ex_d(p).start()

    def d_done(p):
        ex_d(p).wait()
        tot[c] = ss[p]
        tot[oc] = rd[p]

    ex_a(0).start()

    mask[...] = 1.0 - dot(et[...], jnp.ones((IFACE, CASES), BF16))

    def columns_of_interface(i, _):
        rows = slice(i * 512, (i + 1) * 512)
        columns = dot(a[rows, :], et[...])
        ac[rows, :] = columns.astype(BF16)
        for j in range(2):
            lanes = slice(j * CASES, (j + 1) * CASES)
            w[1, rows, lanes] = (columns[:, lanes] * mask[rows, :]).astype(BF16)
        return 0

    for i in range(4):
        columns_of_interface(i, 0)
    a_to_b(0)
    kv = dot(ai[...], w[1])
    q[1, 0] = kv[:, :CASES]
    q[1, 1] = kv[:, CASES:]
    ex_a(1).start()

    def columns_twice(i, _):
        rows = slice(i * 512, (i + 1) * 512)
        gc[rows, :] = dot(a[rows, :], w[1]).astype(BF16)
        return 0

    for i in range(4):
        columns_twice(i, 0)
    a_to_b(1)

    load_sbo.wait()
    load_st.wait()
    swap_st.wait()
    swap_src.wait()
    src[c] = sbo[...]
    src[oc] = rf[...].astype(BF16)
    for j in range(2):
        w[0, :, j * CASES:(j + 1) * CASES] = (st[j] + src[j].astype(F32)).astype(BF16)
        sI[:, j * CASES:(j + 1) * CASES] = dot(e[...], src[j])
    bq[...] = dot(aii.astype(BF16), sI[...].astype(BF16))

    def constant_source(i, _):
        rows = slice(i * 512, (i + 1) * 512)
        fixed = dot(ac[rows, :], sI[...].astype(BF16))
        for j in range(2):
            lanes = slice(j * CASES, (j + 1) * CASES)
            sg[j, rows, :] = fixed[:, lanes]
        return 0

    for i in range(4):
        constant_source(i, 0)
    for ref in (k0h, k0l, k1h, k1l, m1h, m1l, m2h, m2l):
        ref[...] = jnp.zeros_like(ref)

    def decay_wait(j, _):
        decay_out(j).wait_send()
        decay_in(j).wait_recv()
        return 0

    lax.fori_loop(1, SLABS, decay_wait, 0)
    b_to_c(0)

    def total():
        return jnp.concatenate([tot[0], tot[1]], axis=1) * (1.0 / SUBS)

    def next_mean():
        mean = dot(k0h[...], m1h[...]) + dot(k0h[...], m1l[...]) + dot(k0l[...], m1h[...])
        mean += dot(k1h[...], m2h[...]) + dot(k1h[...], m2l[...]) + dot(k1l[...], m2h[...])
        return mean + total()

    def push_mean():
        mean = next_mean()
        m2h[...] = m1h[...]
        m2l[...] = m1l[...]
        high, low = split2(mean)
        m1h[...] = high
        m1l[...] = low
        return mean

    after = jnp.minimum(2 * m + 2, SLABS - 1)

    def step(k, _):
        p, pn = lax.rem(k, 2), lax.rem(k + 1, 2)
        now, next1, next2 = lax.rem(k, SLOTS), lax.rem(k + 1, SLOTS), lax.rem(k + 2, SLOTS)
        later = jnp.where(k > 0, 1.0, 0.0)
        qv = dot(ai[...], w[p]) + later * bq[...]
        q[next2, 0] = qv[:, :CASES]
        q[next2, 1] = qv[:, CASES:]
        ex_a(next2).start()
        def part(i):
            z[i * 512:(i + 1) * 512, :] = dot(a[i * 512:(i + 1) * 512, :], w[p])

        part(0)
        part(1)
        a_to_b(next2)
        b_to_c(next1)
        c_to_d(now)
        part(2)
        for i in range(2):
            b = 2 * k + i
            dcol[0, block(b, 128), :] = column(decall[2 * m, pl.ds(b, 1), :])
            dcol[1, block(b, 128), :] = column(decall[2 * m + 1, pl.ds(b, 1), :])
            dcol[2, block(b, 128), :] = column(decall[after, pl.ds(b, 1), :])
            dpk[b] = column(decall[2 * b, pl.ds(m, 1), :] * decall[2 * b + 1, pl.ds(m, 1), :])
        part(3)
        d_done(now)

        @pl.when(k == 0)
        def _():
            high, low = split2(total())
            k0h[...] = high
            k0l[...] = low

        @pl.when(k == 1)
        def _():
            high, low = split2(total())
            k1h[...] = high
            k1l[...] = low

        @pl.when(k > 1)
        def _():
            push_mean()

        for i in range(4):
            rows = slice(i * 512, (i + 1) * 512)
            more = dot(gc[rows, :], m1h[...])
            for j in range(2):
                lanes = slice(j * CASES, (j + 1) * CASES)
                zf = z[rows, lanes] + more[:, lanes] + later * sg[j, rows, :]
                z[rows, lanes] = zf
                w[pn, rows, lanes] = (mask[rows, :] * (zf + src[j, rows, :].astype(F32))).astype(BF16)
        return 0

    lax.fori_loop(0, STEPS, step, 0)

    now, next1 = STEPS % SLOTS, (STEPS + 1) % SLOTS
    c_to_d(now)
    b_to_c(next1)
    d_done(now)
    push_mean()

    def last_columns(i, _):
        rows = slice(i * 512, (i + 1) * 512)
        z[rows, :] += dot(ac[rows, :], m1h[...])
        return 0

    for i in range(4):
        last_columns(i, 0)
    c_to_d(next1)
    d_done(next1)
    mean = next_mean()
    p1, rest = mean.astype(BF16), mean - mean.astype(BF16).astype(F32)
    p2, p3 = split2(rest)
    k0h[...] = p1
    k0l[...] = p2
    k1h[...] = p3

    def to_chip(o):
        t = lax.rem(m + o, CHIPS)
        return t, (2 * t + c, u)

    def in_out(o):
        t, there = to_chip(o)
        return remote(cs.at[block(t, PIECE)], inbox.at[m], tis.at[o], tir.at[m], there)

    def in_in(o):
        t, there = to_chip(o)
        return remote(cs.at[block(t, PIECE)], inbox.at[t], tis.at[o], tir.at[t], there)

    back = lax.rem(m + CHIPS - 1, CHIPS)

    def shift(t):
        rows = block(t, PIECE)
        return remote(cc.at[0, rows], c2.at[rows], shs.at[t], shr.at[t], (2 * back + c, u))

    def corrections(o, _):
        t = lax.rem(m + o, CHIPS)
        rows = block(t, PIECE)
        spread = dot(et[rows, :], k0h[...]) + dot(et[rows, :], k0l[...]) + dot(et[rows, :], k1h[...])
        f0 = z[rows, :CASES] * mask[rows, :] + spread[:, :CASES]
        f1 = z[rows, CASES:] * mask[rows, :] + spread[:, CASES:]
        c0 = f0 - dcol[0, rows, :] * st[0, rows, :]
        c1 = f1 - dcol[1, rows, :] * st[1, rows, :]
        cc[0, rows, :] = c0
        cc[1, rows, :] = c1
        cs[rows, :] = dcol[1, rows, :] * jnp.where(m == 0, f0, c0) + c1

        @pl.when(o < CHIPS)
        def _():
            in_out(o).start()

        @pl.when(jnp.logical_or(o <= EARLY, o == CHIPS))
        def _():
            shift(t).start()

        return 0

    lax.fori_loop(1, CHIPS + 1, corrections, 0)
    inbox[m] = cs[block(m, PIECE), :]

    def in_wait(o, _):
        in_out(o).wait_send()
        in_in(o).wait_recv()
        return 0

    lax.fori_loop(1, CHIPS, in_wait, 0)

    retire = ret_ref[...]

    def scan(k, state):
        new = dpk[k] * state + inbox[k]
        outbox[k] = jnp.where(retire >= 2, new, state)
        return new

    lax.fori_loop(0, CHIPS, scan, jnp.zeros((PIECE, CASES), F32))

    def back_out(o):
        t, there = to_chip(o)
        return remote(outbox.at[t], yb.at[block(m, PIECE)], tos.at[o], tor.at[m], there)

    def back_in(o):
        t, there = to_chip(o)
        return remote(outbox.at[t], yb.at[block(t, PIECE)], tos.at[o], tor.at[t], there)

    def back_go(o, _):
        back_out(o).start()

        @pl.when(o < CHIPS - EARLY)
        def _():
            shift(lax.rem(m + CHIPS - o, CHIPS)).start()

        return 0

    lax.fori_loop(1, CHIPS, back_go, 0)
    yb[block(m, PIECE), :] = outbox[m]

    def to_mate(j):
        rows = block(j, PIECE)
        return remote(ws.at[rows], rw.at[rows], ws_.at[j], wr_.at[j], mate)

    last = m == CHIPS - 1

    def finish(j):
        rows = block(j, PIECE)
        shift(j).wait_recv()
        got = yb[rows, :]
        zero = jnp.logical_and(m == 0, retire < 2)
        got = jnp.where(zero, st[0, rows, :], got)
        v1 = dcol[0, rows, :] * got + cc[0, rows, :]
        v2 = dcol[1, rows, :] * v1 + cc[1, rows, :]
        v3 = jnp.where(last, got, dcol[2, rows, :] * got + c2[rows, :])
        w0 = jnp.where(retire == 1, v1, got)
        w1 = jnp.where(retire == 0, v1, jnp.where(retire == 1, v2, v3))
        ob[rows, :] = jnp.where(c == 0, w0, w1)
        ws[rows, :] = jnp.where(c == 0, w1, w0)
        to_mate(j).start()

    finish(m)

    def finish_at(o, _):
        t = lax.rem(m + CHIPS - o, CHIPS)
        back_in(CHIPS - o).wait_recv()
        finish(t)
        return 0

    lax.fori_loop(1, CHIPS, finish_at, 0)
    store_own = pltpu.make_async_copy(ob, out_ref.at[c], lsem.at[0])
    store_own.start()

    def last_waits(j, _):
        to_mate(j).wait()
        shift(j).wait_send()
        return 0

    lax.fori_loop(0, CHIPS, last_waits, 0)
    store_other = pltpu.make_async_copy(rw, out_ref.at[oc], lsem.at[1])
    store_other.start()

    def back_sent(o, _):
        back_out(o).wait_send()
        return 0

    lax.fori_loop(1, CHIPS, back_sent, 0)
    store_own.wait()
    store_other.wait()


def body(starts, sources, inverse_conductance, coarse_decay, interface_nodes, retire):
    hbm = pl.BlockSpec(memory_space=pl.ANY)
    vmem = pl.BlockSpec(memory_space=pltpu.VMEM)
    V, D = pltpu.VMEM, pltpu.SemaphoreType.DMA
    whole = (NODES, CASES)
    wide = (NODES, 2 * CASES)
    ifw = (IFACE, 2 * CASES)
    ex = (2, IFACE, CASES)
    scratch = [
        V((2, 16, 128), F32), V((NODES, NODES), BF16), V((IFACE, NODES), BF16), V((NODES, IFACE), BF16),
        V((IFACE, NODES), BF16), V((NODES, IFACE), BF16),
        V((2,) + wide, BF16), V(wide, F32), V((2,) + whole, BF16), V((2,) + whole, F32),
        V(whole, BF16), V(whole, BF16), V(whole, F32), V(whole, F32), V(whole, F32),
        V((3,) + whole, F32), V((CHIPS, PIECE, CASES), F32), V((SLABS, 16, 128), F32),
        V(ifw, F32), V(ifw, F32), V((NODES, IFACE), BF16), V((2,) + whole, F32),
        *[V(ifw, BF16)] * 8, V(ex, F32),
        V((SLOTS,) + ex, F32), *[V((SLOTS, IFACE, CASES), F32)] * 7,
        V((2,) + whole, F32), V(whole, F32), V((CHIPS, PIECE, CASES), F32), V((CHIPS, PIECE, CASES), F32),
        V(whole, F32), V(whole, F32), V(whole, F32), V(whole, F32), V(whole, F32),
        D((3,)), D((4,)), D((2,)), D((2,)), D((SLABS,)), D((SLABS,)),
        D((SLOTS,)), D((SLOTS,)), *[D((SLOTS, 2))] * 4, D((SLOTS,)), D((SLOTS,)),
        D((CHIPS,)), D((CHIPS,)), D((CHIPS,)), D((CHIPS,)), D((CHIPS,)), D((CHIPS,)), D((CHIPS,)), D((CHIPS,)),
    ]
    out = pl.pallas_call(
        kernel,
        out_shape=jax.ShapeDtypeStruct((2,) + whole, F32),
        in_specs=[vmem] * 3 + [hbm] * 3,
        out_specs=hbm,
        scratch_shapes=scratch,
        compiler_params=pltpu.CompilerParams(
            collective_id=0, has_side_effects=True, vmem_limit_bytes=56 << 20
        ),
        cost_estimate=pl.CostEstimate(flops=2 * 9 * 2304 * 2304 * 256, bytes_accessed=16 << 20, transcendentals=0),
        name="parareal",
    )(
        coarse_decay[0],
        interface_nodes,
        retire.reshape(1, CASES),
        starts[0],
        sources[0],
        inverse_conductance,
    )
    return out[None]


def solution(mesh):
    return jax.shard_map(
        body,
        mesh=mesh,
        in_specs=(
            P("slab", "sub", None, None),
            P("slab", "sub", None, None),
            P("sub", None, None),
            P("slab", "sub", None),
            P("sub", None),
            P(),
        ),
        out_specs=P("slab", "sub", None, None),
        check_vma=False,
    )
```

```python
import functools

import jax
import jax.numpy as jnp
from jax import lax
from jax.experimental import pallas as pl
from jax.experimental.pallas import tpu as pltpu
from jax.sharding import PartitionSpec as P

NODES = 2048
CASES = 128
IFACE = 256
STEPS = 8
SUBS = 8
SLABS = 32
CHIPS = SLABS // 2
PIECE = NODES // CHIPS
HALF = IFACE // 2
EARLY = 6
SLOTS = 3
MESH = pl.DeviceIdType.MESH
F32, BF16 = jnp.float32, jnp.bfloat16


def dot(a, b):
    return jnp.dot(a, b, preferred_element_type=F32)


def split2(value):
    high = value.astype(BF16)
    return high, (value - high.astype(F32)).astype(BF16)


def block(index, size):
    return pl.ds(pl.multiple_of(index * size, size), size)


def column(row):
    return jnp.broadcast_to(row, (128, 128)).T


def kernel(
    decay_ref, idx_ref, ret_ref, starts_ref, sources_ref, cond_ref,
    out_ref,
    dec_ref, a, e, et, ai, ac, w, z, src, st, sbo, sbx, sf, rf, mask, dcol, dpk, decall,
    sI, bq, gc, sg, k0h, k0l, k1h, k1l, m1h, m1l, m2h, m2l, tot,
    q, ra, h, rb, hb, rc, ss, rd,
    cc, cs, inbox, outbox, yb, c2, ws, rw, ob,
    lsem, asem, swsem, swrec, dsend, drecv,
    as_, ar_, bs_, br_, cs_, cr_, ds_, dr_,
    tis, tir, tos, tor, shs, shr, ws_, wr_,
):
    s, u = lax.axis_index("slab"), lax.axis_index("sub")
    c = lax.rem(s, 2)
    m = lax.div(s, 2)
    oc = 1 - c
    mate = (s + 1 - 2 * c, u)
    first = (s, u + 1 - 2 * lax.rem(u, 2))
    second = (s, 3 - u)

    loads = [
        pltpu.make_async_copy(cond_ref.at[c, pl.ds(i * 512, 512)], a.at[pl.ds(i * 512, 512)], asem.at[i])
        for i in range(4)
    ]
    load_sbx = pltpu.make_async_copy(sources_ref.at[oc], sbx, lsem.at[0])
    load_sbo = pltpu.make_async_copy(sources_ref.at[c], sbo, lsem.at[1])
    load_st = pltpu.make_async_copy(starts_ref.at[c], st.at[c], lsem.at[2])
    load_sbx.start()
    for load in loads:
        load.start()
    load_sbo.start()
    load_st.start()

    barrier = pltpu.get_barrier_semaphore()

    def greet(j, _):
        pl.semaphore_signal(barrier, inc=1, device_id=(lax.rem(s + j, SLABS), u), device_id_type=MESH)
        return 0

    lax.fori_loop(1, SLABS, greet, 0)
    pl.semaphore_signal(barrier, inc=1, device_id=first, device_id_type=MESH)
    pl.semaphore_signal(barrier, inc=1, device_id=second, device_id_type=MESH)

    for j in range(2):
        for b in range(16):
            dec_ref[j, b:b + 1, :] = decay_ref[j:j + 1, b * 128:(b + 1) * 128]
    nodes_at = idx_ref[pl.ds(c, 1), :].astype(F32)
    et[...] = (lax.broadcasted_iota(jnp.int32, (NODES, IFACE), 0).astype(F32) == nodes_at).astype(F32).astype(BF16)
    lane = lax.broadcasted_iota(jnp.int32, (128, 128), 1).astype(F32)
    for i in range(2):
        nodes_down = column(nodes_at[:, i * 128:(i + 1) * 128])
        for b in range(16):
            e[i * 128:(i + 1) * 128, b * 128:(b + 1) * 128] = (lane + float(b * 128) == nodes_down).astype(F32).astype(BF16)

    for load in loads:
        load.wait()
    for i in range(4):
        ai[:, i * 512:(i + 1) * 512] = dot(e[...], a[:, i * 512:(i + 1) * 512]).astype(BF16)
    pl.semaphore_wait(barrier, SLABS + 1)

    def remote(source, target, send, receive, to):
        return pltpu.make_async_remote_copy(
            src_ref=source, dst_ref=target, send_sem=send, recv_sem=receive,
            device_id=to, device_id_type=MESH,
        )

    swap_st = remote(starts_ref.at[oc], st.at[c], swsem.at[0], swrec.at[0], mate)
    swap_st.start()
    load_sbx.wait()
    sf[...] = sbx[...].astype(F32)
    swap_src = remote(sf, rf, swsem.at[1], swrec.at[1], mate)
    swap_src.start()

    def decay_out(j):
        t = lax.rem(s + j, SLABS)
        return remote(dec_ref.at[lax.rem(t, 2)], decall.at[s], dsend.at[j], drecv.at[s], (t, u))

    def decay_in(j):
        t = lax.rem(s + j, SLABS)
        return remote(dec_ref.at[c], decall.at[t], dsend.at[j], drecv.at[t], (t, u))

    def go(make):
        def one(j, _):
            make(j).start()
            return 0
        return one

    lax.fori_loop(1, SLABS, go(decay_out), 0)
    decall[s] = dec_ref[c]

    aii = dot(ai[...], et[...])
    q[0, 0] = aii[:, :CASES]
    q[0, 1] = aii[:, CASES:]

    def ex_a(p):
        return remote(q.at[p, oc], ra.at[p], as_.at[p], ar_.at[p], mate)

    def ex_b(p):
        return [
            remote(h.at[p, pl.ds(0, HALF)], rb.at[p, pl.ds(0, HALF)], bs_.at[p, 0], br_.at[p, 0], first),
            remote(h.at[p, pl.ds(HALF, HALF)], rb.at[p, pl.ds(HALF, HALF)], bs_.at[p, 1], br_.at[p, 1], second),
        ]

    def ex_c(p):
        return [
            remote(hb.at[p, pl.ds(0, HALF)], rc.at[p, pl.ds(0, HALF)], cs_.at[p, 0], cr_.at[p, 0], second),
            remote(hb.at[p, pl.ds(HALF, HALF)], rc.at[p, pl.ds(HALF, HALF)], cs_.at[p, 1], cr_.at[p, 1], first),
        ]

    def ex_d(p):
        return remote(ss.at[p], rd.at[p], ds_.at[p], dr_.at[p], mate)

    def a_to_b(p):
        ex_a(p).wait()
        h[p] = q[p, c] + ra[p]
        for copy in ex_b(p):
            copy.start()

    def b_to_c(p):
        for copy in ex_b(p):
            copy.wait()
        hb[p] = h[p] + rb[p]
        for copy in ex_c(p):
            copy.start()

    def c_to_d(p):
        for copy in ex_c(p):
            copy.wait()
        ss[p] = hb[p] + rc[p]
        ex_d(p).start()

    def d_done(p):
        ex_d(p).wait()
        tot[c] = ss[p]
        tot[oc] = rd[p]

    ex_a(0).start()

    mask[...] = 1.0 - dot(et[...], jnp.ones((IFACE, CASES), BF16))

    def columns_of_interface(i, _):
        rows = slice(i * 512, (i + 1) * 512)
        columns = dot(a[rows, :], et[...])
        ac[rows, :] = columns.astype(BF16)
        for j in range(2):
            lanes = slice(j * CASES, (j + 1) * CASES)
            w[1, rows, lanes] = (columns[:, lanes] * mask[rows, :]).astype(BF16)
        return 0

    for i in range(4):
        columns_of_interface(i, 0)
    a_to_b(0)
    kv = dot(ai[...], w[1])
    q[1, 0] = kv[:, :CASES]
    q[1, 1] = kv[:, CASES:]
    ex_a(1).start()

    def columns_twice(i, _):
        rows = slice(i * 512, (i + 1) * 512)
        gc[rows, :] = dot(a[rows, :], w[1]).astype(BF16)
        return 0

    for i in range(4):
        columns_twice(i, 0)
    a_to_b(1)

    load_sbo.wait()
    load_st.wait()
    swap_st.wait()
    swap_src.wait()
    src[c] = sbo[...]
    src[oc] = rf[...].astype(BF16)
    for j in range(2):
        w[0, :, j * CASES:(j + 1) * CASES] = (st[j] + src[j].astype(F32)).astype(BF16)
        sI[:, j * CASES:(j + 1) * CASES] = dot(e[...], src[j])
    bq[...] = dot(aii.astype(BF16), sI[...].astype(BF16))

    def constant_source(i, _):
        rows = slice(i * 512, (i + 1) * 512)
        fixed = dot(ac[rows, :], sI[...].astype(BF16))
        for j in range(2):
            lanes = slice(j * CASES, (j + 1) * CASES)
            sg[j, rows, :] = fixed[:, lanes]
        return 0

    for i in range(4):
        constant_source(i, 0)
    for ref in (k0h, k0l, k1h, k1l, m1h, m1l, m2h, m2l):
        ref[...] = jnp.zeros_like(ref)

    def decay_wait(j, _):
        decay_out(j).wait_send()
        decay_in(j).wait_recv()
        return 0

    lax.fori_loop(1, SLABS, decay_wait, 0)
    b_to_c(0)

    def total():
        return jnp.concatenate([tot[0], tot[1]], axis=1) * (1.0 / SUBS)

    def next_mean():
        mean = dot(k0h[...], m1h[...]) + dot(k0h[...], m1l[...]) + dot(k0l[...], m1h[...])
        mean += dot(k1h[...], m2h[...]) + dot(k1h[...], m2l[...]) + dot(k1l[...], m2h[...])
        return mean + total()

    def push_mean():
        mean = next_mean()
        m2h[...] = m1h[...]
        m2l[...] = m1l[...]
        high, low = split2(mean)
        m1h[...] = high
        m1l[...] = low
        return mean

    after = jnp.minimum(2 * m + 2, SLABS - 1)

    def step(k, _):
        p, pn = lax.rem(k, 2), lax.rem(k + 1, 2)
        now, next1, next2 = lax.rem(k, SLOTS), lax.rem(k + 1, SLOTS), lax.rem(k + 2, SLOTS)
        later = jnp.where(k > 0, 1.0, 0.0)
        qv = dot(ai[...], w[p]) + later * bq[...]
        q[next2, 0] = qv[:, :CASES]
        q[next2, 1] = qv[:, CASES:]
        ex_a(next2).start()
        def part(i):
            z[i * 512:(i + 1) * 512, :] = dot(a[i * 512:(i + 1) * 512, :], w[p])

        part(0)
        part(1)
        a_to_b(next2)
        b_to_c(next1)
        c_to_d(now)
        part(2)
        for i in range(2):
            b = 2 * k + i
            dcol[0, block(b, 128), :] = column(decall[2 * m, pl.ds(b, 1), :])
            dcol[1, block(b, 128), :] = column(decall[2 * m + 1, pl.ds(b, 1), :])
            dcol[2, block(b, 128), :] = column(decall[after, pl.ds(b, 1), :])
            dpk[b] = column(decall[2 * b, pl.ds(m, 1), :] * decall[2 * b + 1, pl.ds(m, 1), :])
        part(3)
        d_done(now)

        @pl.when(k == 0)
        def _():
            high, low = split2(total())
            k0h[...] = high
            k0l[...] = low

        @pl.when(k == 1)
        def _():
            high, low = split2(total())
            k1h[...] = high
            k1l[...] = low

        @pl.when(k > 1)
        def _():
            push_mean()

        for i in range(4):
            rows = slice(i * 512, (i + 1) * 512)
            more = dot(gc[rows, :], m1h[...])
            for j in range(2):
                lanes = slice(j * CASES, (j + 1) * CASES)
                zf = z[rows, lanes] + more[:, lanes] + later * sg[j, rows, :]
                z[rows, lanes] = zf
                w[pn, rows, lanes] = (mask[rows, :] * (zf + src[j, rows, :].astype(F32))).astype(BF16)
        return 0

    lax.fori_loop(0, STEPS, step, 0)

    now, next1 = STEPS % SLOTS, (STEPS + 1) % SLOTS
    c_to_d(now)
    b_to_c(next1)
    d_done(now)
    push_mean()

    def last_columns(i, _):
        rows = slice(i * 512, (i + 1) * 512)
        z[rows, :] += dot(ac[rows, :], m1h[...])
        return 0

    for i in range(4):
        last_columns(i, 0)

    def without_last_mean(i, _):
        rows = block(i, 256)
        for j in range(2):
            lanes = slice(j * CASES, (j + 1) * CASES)
            cc[j, rows, :] = z[rows, lanes] * mask[rows, :] - dcol[j, rows, :] * st[j, rows, :]
        return 0

    lax.fori_loop(0, NODES // 256, without_last_mean, 0)
    c_to_d(next1)
    d_done(next1)
    mean = next_mean()
    p1, rest = mean.astype(BF16), mean - mean.astype(BF16).astype(F32)
    p2, p3 = split2(rest)
    k0h[...] = p1
    k0l[...] = p2
    k1h[...] = p3

    def to_chip(o):
        t = lax.rem(m + o, CHIPS)
        return t, (2 * t + c, u)

    def in_out(o):
        t, there = to_chip(o)
        return remote(cs.at[block(t, PIECE)], inbox.at[m], tis.at[o], tir.at[m], there)

    def in_in(o):
        t, there = to_chip(o)
        return remote(cs.at[block(t, PIECE)], inbox.at[t], tis.at[o], tir.at[t], there)

    back = lax.rem(m + CHIPS - 1, CHIPS)

    def shift(t):
        rows = block(t, PIECE)
        return remote(cc.at[0, rows], c2.at[rows], shs.at[t], shr.at[t], (2 * back + c, u))

    def corrections(o, _):
        t = lax.rem(m + o, CHIPS)
        rows = block(t, PIECE)
        spread = dot(et[rows, :], k0h[...]) + dot(et[rows, :], k0l[...]) + dot(et[rows, :], k1h[...])
        c0 = cc[0, rows, :] + spread[:, :CASES]
        c1 = cc[1, rows, :] + spread[:, CASES:]
        f0 = c0 + dcol[0, rows, :] * st[0, rows, :]
        cc[0, rows, :] = c0
        cc[1, rows, :] = c1
        cs[rows, :] = dcol[1, rows, :] * jnp.where(m == 0, f0, c0) + c1

        @pl.when(o < CHIPS)
        def _():
            in_out(o).start()

        @pl.when(jnp.logical_or(o <= EARLY, o == CHIPS))
        def _():
            shift(t).start()

        return 0

    lax.fori_loop(1, CHIPS + 1, corrections, 0)
    inbox[m] = cs[block(m, PIECE), :]

    def in_wait(o, _):
        in_out(o).wait_send()
        in_in(o).wait_recv()
        return 0

    lax.fori_loop(1, CHIPS, in_wait, 0)

    retire = ret_ref[...]

    def scan(k, state):
        new = dpk[k] * state + inbox[k]
        outbox[k] = jnp.where(retire >= 2, new, state)
        return new

    lax.fori_loop(0, CHIPS, scan, jnp.zeros((PIECE, CASES), F32))

    def back_out(o):
        t, there = to_chip(o)
        return remote(outbox.at[t], yb.at[block(m, PIECE)], tos.at[o], tor.at[m], there)

    def back_in(o):
        t, there = to_chip(o)
        return remote(outbox.at[t], yb.at[block(t, PIECE)], tos.at[o], tor.at[t], there)

    def back_go(o, _):
        back_out(o).start()

        @pl.when(o < CHIPS - EARLY)
        def _():
            shift(lax.rem(m + CHIPS - o, CHIPS)).start()

        return 0

    lax.fori_loop(1, CHIPS, back_go, 0)
    yb[block(m, PIECE), :] = outbox[m]

    def to_mate(j):
        rows = block(j, PIECE)
        return remote(ws.at[rows], rw.at[rows], ws_.at[j], wr_.at[j], mate)

    last = m == CHIPS - 1

    def finish(j):
        rows = block(j, PIECE)
        shift(j).wait_recv()
        got = yb[rows, :]
        zero = jnp.logical_and(m == 0, retire < 2)
        got = jnp.where(zero, st[0, rows, :], got)
        v1 = dcol[0, rows, :] * got + cc[0, rows, :]
        v2 = dcol[1, rows, :] * v1 + cc[1, rows, :]
        v3 = jnp.where(last, got, dcol[2, rows, :] * got + c2[rows, :])
        w0 = jnp.where(retire == 1, v1, got)
        w1 = jnp.where(retire == 0, v1, jnp.where(retire == 1, v2, v3))
        ob[rows, :] = jnp.where(c == 0, w0, w1)
        ws[rows, :] = jnp.where(c == 0, w1, w0)
        to_mate(j).start()

    finish(m)

    def finish_at(o, _):
        t = lax.rem(m + CHIPS - o, CHIPS)
        back_in(CHIPS - o).wait_recv()
        finish(t)
        return 0

    lax.fori_loop(1, CHIPS, finish_at, 0)
    store_own = pltpu.make_async_copy(ob, out_ref.at[c], lsem.at[0])
    store_own.start()

    def last_waits(j, _):
        to_mate(j).wait()
        shift(j).wait_send()
        return 0

    lax.fori_loop(0, CHIPS, last_waits, 0)
    store_other = pltpu.make_async_copy(rw, out_ref.at[oc], lsem.at[1])
    store_other.start()

    def back_sent(o, _):
        back_out(o).wait_send()
        return 0

    lax.fori_loop(1, CHIPS, back_sent, 0)
    store_own.wait()
    store_other.wait()


def body(starts, sources, inverse_conductance, coarse_decay, interface_nodes, retire):
    hbm = pl.BlockSpec(memory_space=pl.ANY)
    vmem = pl.BlockSpec(memory_space=pltpu.VMEM)
    V, D = pltpu.VMEM, pltpu.SemaphoreType.DMA
    whole = (NODES, CASES)
    wide = (NODES, 2 * CASES)
    ifw = (IFACE, 2 * CASES)
    ex = (2, IFACE, CASES)
    scratch = [
        V((2, 16, 128), F32), V((NODES, NODES), BF16), V((IFACE, NODES), BF16), V((NODES, IFACE), BF16),
        V((IFACE, NODES), BF16), V((NODES, IFACE), BF16),
        V((2,) + wide, BF16), V(wide, F32), V((2,) + whole, BF16), V((2,) + whole, F32),
        V(whole, BF16), V(whole, BF16), V(whole, F32), V(whole, F32), V(whole, F32),
        V((3,) + whole, F32), V((CHIPS, PIECE, CASES), F32), V((SLABS, 16, 128), F32),
        V(ifw, F32), V(ifw, F32), V((NODES, IFACE), BF16), V((2,) + whole, F32),
        *[V(ifw, BF16)] * 8, V(ex, F32),
        V((SLOTS,) + ex, F32), *[V((SLOTS, IFACE, CASES), F32)] * 7,
        V((2,) + whole, F32), V(whole, F32), V((CHIPS, PIECE, CASES), F32), V((CHIPS, PIECE, CASES), F32),
        V(whole, F32), V(whole, F32), V(whole, F32), V(whole, F32), V(whole, F32),
        D((3,)), D((4,)), D((2,)), D((2,)), D((SLABS,)), D((SLABS,)),
        D((SLOTS,)), D((SLOTS,)), *[D((SLOTS, 2))] * 4, D((SLOTS,)), D((SLOTS,)),
        D((CHIPS,)), D((CHIPS,)), D((CHIPS,)), D((CHIPS,)), D((CHIPS,)), D((CHIPS,)), D((CHIPS,)), D((CHIPS,)),
    ]
    out = pl.pallas_call(
        kernel,
        out_shape=jax.ShapeDtypeStruct((2,) + whole, F32),
        in_specs=[vmem] * 3 + [hbm] * 3,
        out_specs=hbm,
        scratch_shapes=scratch,
        compiler_params=pltpu.CompilerParams(
            collective_id=0, has_side_effects=True, vmem_limit_bytes=56 << 20
        ),
        cost_estimate=pl.CostEstimate(flops=2 * 9 * 2304 * 2304 * 256, bytes_accessed=16 << 20, transcendentals=0),
        name="parareal",
    )(
        coarse_decay[0],
        interface_nodes,
        retire.reshape(1, CASES),
        starts[0],
        sources[0],
        inverse_conductance,
    )
    return out[None]


def solution(mesh):
    return jax.shard_map(
        body,
        mesh=mesh,
        in_specs=(
            P("slab", "sub", None, None),
            P("slab", "sub", None, None),
            P("sub", None, None),
            P("slab", "sub", None),
            P("sub", None),
            P(),
        ),
        out_specs=P("slab", "sub", None, None),
        check_vma=False,
    )
```
